32 devices in a mesh: ctx: 8 (over z, core), exp: 4 (over y, x).
Axes of the slice: x: 2, y: 2, z: 4, core: 2. Of those that a mesh axis runs over, the one named last changes fastest.
Arguments:
- queries: bfloat16 [4, 2048, 2048], P('exp', 'ctx'), may hold values from -64 to 64
- keys: bfloat16 [4, 2048, 256], P('exp', 'ctx'), may hold values from -6 to 6
- values: bfloat16 [4, 2048, 256], P('exp', 'ctx'), may hold values from -6 to 6
- hidden_in: bfloat16 [4, 2048, 2048], P('exp', 'ctx'), may hold values from -60 to 60
- out_proj: bfloat16 [2048, 2048], replicated, may hold values from -1.5 to 1.5
- norm_gain: float32 [2048], replicated, may hold values from 0.1 to 1.9
- route_ids: int32 [4, 2048, 8], P('exp', 'ctx'), may hold values from 0 to 31, all different within a row; in each aligned block of 256 rows (0 to 255, 256 to 511, ..., all dimensions but the last counted through in order) at most 128 rows name the same one
- route_scores: float32 [4, 2048, 8], P('exp', 'ctx'), may hold values from -310 to 310
- expert_weights: bfloat16 [32, 3, 2048, 768], P(('ctx', 'exp')), may hold values from -0.25 to 0.25
Outputs:
- residual_out: bfloat16 [4, 2048, 2048], P('exp', 'ctx')
- layer_out: bfloat16 [4, 2048, 2048], P('exp', 'ctx')
The draws below stay inside these ranges and needn't reach their ends.
Inputs may be any that keep to these rules, and one draw needn't show every extreme that they name: `route_ids`: each row names 8 different experts. In each aligned block of 256 rows (the rows of one device) no expert is named by more than 128 rows.
All inputs are finite; a program needn't handle non-finite values.
Results may differ from the reference program's by a relative error of at most 0.023.
Values may be sent and summed in bfloat16 or wider, within the bound.
A program may use at most 192 MiB of HBM per device.

```python
import math
import jax
import jax.numpy as jnp
import numpy as np
from jax import lax

D = 2048
HEADS = 16
KV_HEADS = 2
HEAD_DIM = 128
FF = 768
TOP = 8
TOK_DEV = 256
EXPERTS = 32
CAP = 128
SEQS = 4
LENGTH = 2048


def drawn_pair(key):
    base = jax.random.fold_in(key, 31)
    k_query, k_key = jax.random.split(base, 2)
    query_all = 1.5 * jax.random.truncated_normal(k_query, -6.0, 6.0, (SEQS, LENGTH, HEADS, HEAD_DIM), jnp.float32)
    key_all = jax.random.truncated_normal(k_key, -6.0, 6.0, (SEQS, LENGTH, KV_HEADS, HEAD_DIM), jnp.float32)
    return (query_all.reshape(SEQS, LENGTH, HEADS * HEAD_DIM), key_all.reshape(SEQS, LENGTH, KV_HEADS * HEAD_DIM))


def draw_queries(key, part):
    return drawn_pair(key)[0].astype(jnp.bfloat16)


def draw_keys(key, part):
    return drawn_pair(key)[1].astype(jnp.bfloat16)


def draw_hidden_in(key, part):
    k_noise, k_column, k_row = jax.random.split(jax.random.fold_in(key, 5), 3)
    noise = jax.random.truncated_normal(k_noise, -5.0, 5.0, (SEQS, LENGTH, D), jnp.float32)
    columns = jnp.exp(jax.random.uniform(k_column, (D,), jnp.float32, math.log(0.3), math.log(3.0)))
    row_scale = jnp.exp(jax.random.uniform(k_row, (SEQS, LENGTH, 1), jnp.float32, math.log(0.3), math.log(3.0)))
    result = noise * columns * row_scale
    return result.astype(jnp.bfloat16)


def draw_route_scores(key, part):
    k_base = jax.random.fold_in(jax.random.fold_in(key, 9), 0)
    result = 0.5 * jax.random.truncated_normal(k_base, -4.0, 4.0, (SEQS, LENGTH, TOP), jnp.float32)
    return result


def block_scale(key, dims, cuts, low, high):
    factor_of = 1.0
    for dim, shards_of in cuts:
        heights = jax.random.uniform(jax.random.fold_in(jax.random.fold_in(key, 6), dim), (shards_of,), jnp.float32, low / len(cuts), high / len(cuts))
        factor_of = factor_of * jnp.repeat(jnp.exp(heights), dims[dim] // shards_of).reshape((-1,) + (1,) * (len(dims) - 1 - dim))
    return factor_of


def routed_block(key, own, number, rows, number_of, top, reach, skew):
    order = jax.random.permutation(key, number_of)
    packed, usual = portions_of(number_of, rows * top, reach, skew, True), portions_of(number_of, rows * top, reach, skew, False)
    places = jnp.arange(number_of)

    def named(tallies, rotation):
        used = int((tallies > 0).sum())
        fixed = max(1, used // 4)
        shifted = fixed + (places - fixed + rotation * (used - fixed)) % max(1, number_of - fixed)
        return jnp.zeros((number_of,), jnp.int32).at[order[jnp.where(places < fixed, places, shifted)]].set(jnp.asarray(tallies, jnp.int32))

    tallies = jnp.where(number % 4 == 0, named(packed, number // 4), named(usual, number - number // 4 - 1))
    mixed = jax.random.permutation(jax.random.fold_in(own, 3), number_of)
    source_of, taker = mixed[0:number_of // 2 * 2:2], mixed[1:number_of // 2 * 2:2]
    slack = jnp.minimum(tallies[source_of] - 1, reach - tallies[taker]) // 2
    slack = jnp.where((source_of == order[0]) | (taker == order[0]) | (tallies[taker] == 0), 0, jnp.maximum(slack, 0))
    shifted = jax.random.randint(jax.random.fold_in(own, 4), (number_of // 2,), 0, 1 << 20) % (slack + 1)
    tallies = tallies.at[source_of].add(-shifted).at[taker].add(shifted)
    labels = jnp.searchsorted(jnp.cumsum(tallies), jnp.arange(rows * top), side="right").astype(jnp.int32)
    grid = labels.reshape(top, rows).T
    grid = grid[jax.random.permutation(jax.random.fold_in(own, 1), rows)]
    rotation = jax.random.randint(jax.random.fold_in(own, 2), (rows, 1), 0, top)
    return jnp.take_along_axis(grid, (jnp.arange(top)[None, :] + rotation) % top, axis=1)


def portions_of(count, total, bound, slope, full):
    weights = [(1 << 20) // math.isqrt(standing ** slope) + 1 for standing in range(1, count + 1)]
    largest = bound if full else min(bound, max(-(-total // count), total * weights[0] // sum(weights)))
    least = 1 if total - largest >= count - 1 else 0
    given, surplus = [largest] + [least] * (count - 1), total - largest - least * (count - 1)
    while surplus > 0:
        movable = [i for i in range(1, count) if given[i] < largest] or [i for i in range(1, count) if given[i] < bound]
        pool, remaining = sum([weights[i] for i in movable]), surplus
        for i in movable:
            more = min(bound - given[i], max(1, remaining * weights[i] // pool), surplus)
            given[i] = given[i] + more
            surplus = surplus - more
    return np.array(given)


def gaussian(own_key, shape, deviation, most, pieces=(), held_as=jnp.bfloat16):
    loudness = block_scale(own_key, shape, pieces, -0.22, 0.18) if pieces else 1.0
    array = jax.random.normal(own_key, shape, jnp.float32) * deviation * loudness
    return jnp.minimum(jnp.maximum(array, -most), most).astype(held_as)


def setup_inputs(seed: int = 0) -> dict:
    arg_keys = jax.random.split(jax.random.key(seed), 10)
    queries = draw_queries(jax.random.fold_in(arg_keys[9], 71), 0)
    keys = draw_keys(jax.random.fold_in(arg_keys[9], 71), 0)
    values = gaussian(arg_keys[2], (SEQS, LENGTH, KV_HEADS * HEAD_DIM), 1.0, 6.0, ((0, 4), (1, 8)))
    hidden_in = draw_hidden_in(jax.random.fold_in(arg_keys[9], 71), 0)
    out_proj = gaussian(arg_keys[4], (HEADS * HEAD_DIM, D), 16 ** -0.5, 1.5)
    norm_gain = jnp.clip(1.0 + 0.18 * jax.random.normal(arg_keys[5], (D,), jnp.float32), 0.1, 1.9)
    route_ids_keys = jax.random.split(jax.random.fold_in(arg_keys[6], 1), SEQS * LENGTH // TOK_DEV)
    route_ids_turns = jax.random.permutation(jax.random.fold_in(arg_keys[6], 3), SEQS * LENGTH // TOK_DEV)
    route_ids = jax.vmap(lambda own, number: routed_block(jax.random.fold_in(arg_keys[6], 2), own, number, TOK_DEV, EXPERTS, TOP, CAP, 2))(route_ids_keys, route_ids_turns).reshape((SEQS, LENGTH, TOP))
    route_scores = draw_route_scores(jax.random.fold_in(arg_keys[9], 71), 0)
    expert_weights = gaussian(arg_keys[8], (EXPERTS, 3, D, FF), (D // 4) ** -0.5, 0.25, ((0, 32),))
    return dict(queries=queries, keys=keys, values=values, hidden_in=hidden_in, out_proj=out_proj, norm_gain=norm_gain, route_ids=route_ids, route_scores=route_scores, expert_weights=expert_weights)


def expert_rows(rows, weights):
    gate_part = jnp.dot(rows, weights[0], preferred_element_type=jnp.float32)
    upper_part = jnp.dot(rows, weights[1], preferred_element_type=jnp.float32)
    hidden_rows = (jax.nn.silu(gate_part) * upper_part).astype(jnp.bfloat16)
    result = lax.dot_general(hidden_rows, weights[2], (((1,), (1,)), ((), ())), preferred_element_type=jnp.float32)
    return result.astype(jnp.bfloat16)

def reference(queries, keys, values, hidden_in, out_proj, norm_gain, route_ids, route_scores, expert_weights):
    group_size = HEADS // KV_HEADS
    score_scale = 1.0 / math.sqrt(HEAD_DIM)
    positions = jnp.arange(LENGTH, dtype=jnp.int32)
    causal = positions[None, :] <= positions[:, None]

    def one_sequence(inputs):
        query_seq, key_seq, value_seq = inputs

        def one_head(head):
            kv_head = head // group_size
            query_head = lax.dynamic_slice_in_dim(query_seq, head * HEAD_DIM, HEAD_DIM, 1)
            key_head = lax.dynamic_slice_in_dim(key_seq, kv_head * HEAD_DIM, HEAD_DIM, 1)
            value_head = lax.dynamic_slice_in_dim(value_seq, kv_head * HEAD_DIM, HEAD_DIM, 1)
            scores = jnp.dot(query_head, key_head.T, preferred_element_type=jnp.float32) * score_scale
            scores = jnp.where(causal, scores, -1e+30)
            row_max = scores.max(-1, keepdims=True)
            exps = jnp.where(causal, jnp.exp(scores - row_max), 0.0)
            summed = jnp.dot(exps.astype(jnp.bfloat16), value_head, preferred_element_type=jnp.float32)
            return summed / exps.sum(-1, keepdims=True)
        heads_out = lax.map(one_head, jnp.arange(HEADS, dtype=jnp.int32))
        return heads_out.transpose(1, 0, 2).reshape(LENGTH, HEADS * HEAD_DIM).astype(jnp.bfloat16)
    attended = lax.map(one_sequence, (queries, keys, values))
    total_tokens = SEQS * LENGTH
    projected = jnp.dot(attended.reshape(total_tokens, HEADS * HEAD_DIM), out_proj, preferred_element_type=jnp.float32)
    residual = (hidden_in.reshape(total_tokens, D).astype(jnp.float32) + projected).astype(jnp.bfloat16)
    resid_f = residual.astype(jnp.float32)
    normed = (resid_f * lax.rsqrt(lax.optimization_barrier(jnp.mean(resid_f * resid_f, -1, keepdims=True)) + 1e-06) * norm_gain).astype(jnp.bfloat16)
    gates = jax.nn.softmax(route_scores.astype(jnp.float32), -1)
    expert_ids = route_ids.reshape(-1).astype(jnp.int32)
    gate_flat = gates.reshape(-1)
    pair_count = total_tokens * TOP
    order = jnp.argsort(expert_ids, stable=True).astype(jnp.int32)
    loads = jnp.zeros((EXPERTS,), jnp.int32).at[expert_ids].add(1)
    starts = (jnp.cumsum(loads) - loads).astype(jnp.int32)
    block_rows = 512

    def one_expert(mixture, expert):
        weights = expert_weights[expert]

        def one_block(index, mixture):
            slots = starts[expert] + index * block_rows + jnp.arange(block_rows, dtype=jnp.int32)
            live = slots < starts[expert] + loads[expert]
            pair = order[jnp.minimum(slots, pair_count - 1)]
            token = pair // TOP
            result = expert_rows(normed[token], weights)
            term = jnp.where(live[:, None], gate_flat[pair][:, None] * result.astype(jnp.float32), 0.0)
            return mixture.at[token].add(term)
        turns = (loads[expert] + block_rows - 1) // block_rows
        return (lax.fori_loop(0, turns, one_block, mixture), None)
    mixture, _ = lax.scan(one_expert, jnp.zeros((total_tokens, D), jnp.float32), jnp.arange(EXPERTS, dtype=jnp.int32))
    layer_out = (resid_f + mixture).astype(jnp.bfloat16)
    return (residual.reshape(SEQS, LENGTH, D), layer_out.reshape(SEQS, LENGTH, D))
```

```python
import math

import jax
import jax.numpy as jnp
from jax import lax
from jax.experimental import pallas as pl
from jax.experimental.pallas import tpu as pltpu
from jax.sharding import PartitionSpec as P

D = 2048
HEADS = 16
KV_HEADS = 2
HEAD_DIM = 128
TOP = 8
GROUP = 512
ROUND_TOKENS = 8192


def attend(queries, keys, values):
    tok_rows = queries.shape[1]
    group_size = HEADS // KV_HEADS
    score_scale = 1.0 / math.sqrt(HEAD_DIM)
    query_heads = queries[0].reshape(tok_rows, KV_HEADS, group_size, HEAD_DIM)
    first_row = lax.axis_index("ctx") * tok_rows
    query_pos = first_row + jnp.arange(tok_rows, dtype=jnp.int32)
    last_row = first_row + tok_rows - 1
    running = (
        jnp.full((tok_rows, KV_HEADS, group_size), -1e30, jnp.float32),
        jnp.zeros((tok_rows, KV_HEADS, group_size), jnp.float32),
        jnp.zeros((tok_rows, KV_HEADS, group_size, HEAD_DIM), jnp.float32),
    )
    key_piece = lax.all_gather(keys[0], "ctx", axis=0, tiled=True)
    value_piece = lax.all_gather(values[0], "ctx", axis=0, tiled=True)
    piece_rows = key_piece.shape[0]
    absorb_block_rows = math.gcd(piece_rows, 512)

    def one_block(index, running):
        block_start = index * absorb_block_rows

        def compute(running):
            running_max, denom, accum = running
            key_rows = lax.dynamic_slice_in_dim(
                key_piece, block_start, absorb_block_rows, 0
            ).reshape(absorb_block_rows, KV_HEADS, HEAD_DIM)
            value_rows = lax.dynamic_slice_in_dim(
                value_piece, block_start, absorb_block_rows, 0
            ).reshape(absorb_block_rows, KV_HEADS, HEAD_DIM)
            scores = (
                jnp.einsum(
                    "tgjd,ngd->tgjn", query_heads, key_rows, preferred_element_type=jnp.float32
                )
                * score_scale
            )
            key_pos = block_start + jnp.arange(absorb_block_rows, dtype=jnp.int32)
            visible = (key_pos[None, :] <= query_pos[:, None])[:, None, None, :]
            scores = jnp.where(visible, scores, -1e30)
            new_max = jnp.maximum(running_max, scores.max(-1))
            exps = jnp.where(visible, jnp.exp(scores - new_max[..., None]), 0.0)
            rescale = jnp.exp(running_max - new_max)
            denom = denom * rescale + exps.sum(-1)
            added = jnp.einsum(
                "tgjn,ngd->tgjd",
                exps.astype(jnp.bfloat16),
                value_rows,
                preferred_element_type=jnp.float32,
            )
            accum = accum * rescale[..., None] + added
            return (new_max, denom, accum)

        return lax.cond(block_start <= last_row, compute, lambda state: state, running)

    running_max, denom, accum = lax.fori_loop(
        0, piece_rows // absorb_block_rows, one_block, running
    )
    return (accum / denom[..., None]).reshape(tok_rows, HEADS * HEAD_DIM).astype(jnp.bfloat16)


def expert_kernel(gate_ref, slot_ref, tok_ref, weight_ref, down_ref, out_ref):
    slots = slot_ref[0]
    rows = GROUP // 2
    chosen = slots == lax.broadcasted_iota(jnp.int32, (rows, GROUP), 0)
    row_gates = jnp.sum(jnp.where(chosen, gate_ref[0], 0.0), axis=1, keepdims=True)
    pick = chosen.astype(jnp.float32).astype(jnp.bfloat16)
    tokens = jnp.dot(pick, tok_ref[...], preferred_element_type=jnp.float32).astype(jnp.bfloat16)
    gate_part = jnp.dot(tokens, weight_ref[0, 0], preferred_element_type=jnp.float32)
    upper_part = jnp.dot(tokens, weight_ref[0, 1], preferred_element_type=jnp.float32)
    hidden = (gate_part / (1.0 + jnp.exp(-gate_part)) * upper_part).astype(jnp.bfloat16)
    result = jnp.dot(hidden, down_ref[...], preferred_element_type=jnp.float32)
    scaled = (result.astype(jnp.bfloat16).astype(jnp.float32) * row_gates).astype(jnp.bfloat16)
    out_ref[...] = lax.dot_general(
        pick, scaled, (((0,), (0,)), ((), ())), preferred_element_type=jnp.float32
    ).astype(jnp.bfloat16)


def expert_terms(tokens, gates, slots, weights, down):
    groups = tokens.shape[0] // GROUP
    ff = weights.shape[-1]
    return pl.pallas_call(
        expert_kernel,
        grid=(groups,),
        in_specs=[
            pl.BlockSpec((1, 1, GROUP), lambda i: (i, 0, 0)),
            pl.BlockSpec((1, 1, GROUP), lambda i: (i, 0, 0)),
            pl.BlockSpec((GROUP, D), lambda i: (i, 0)),
            pl.BlockSpec((1, 2, D, ff), lambda i: (0, 0, 0, 0)),
            pl.BlockSpec((ff, D), lambda i: (0, 0)),
        ],
        out_specs=pl.BlockSpec((GROUP, D), lambda i: (i, 0)),
        out_shape=jax.ShapeDtypeStruct(tokens.shape, jnp.bfloat16),
        compiler_params=pltpu.CompilerParams(vmem_limit_bytes=56 * 1024 * 1024),
        cost_estimate=pl.CostEstimate(
            flops=tokens.shape[0] * D * (3 * ff + 2 * GROUP),
            bytes_accessed=4 * tokens.size + 6 * D * ff,
            transcendentals=tokens.shape[0] * ff // 2,
        ),
    )(gates, slots, tokens, weights, down)


def on_device(
    queries, keys, values, hidden_in, out_proj, norm_gain, route_ids, route_scores, expert_weights
):
    tok_rows = queries.shape[1]
    both = ("ctx", "exp")
    n_dev = lax.axis_size("ctx") * lax.axis_size("exp")
    gates = jax.nn.softmax(route_scores[0], -1)
    named = route_ids[0][None, :, :] == jnp.arange(n_dev, dtype=jnp.int32)[:, None, None]
    by_expert = jnp.sum(jnp.where(named, gates[None], 0.0), -1)
    by_expert = jnp.where(jnp.any(named, -1), by_expert, -1.0)
    my_gates = lax.all_to_all(by_expert, both, split_axis=0, concat_axis=0, tiled=True)
    down = expert_weights[0, 2].T

    rounds = n_dev * tok_rows // ROUND_TOKENS
    part_rows = tok_rows // rounds
    groups = ROUND_TOKENS // GROUP
    round_gates = my_gates.reshape(n_dev, rounds, part_rows).transpose(1, 0, 2)
    round_gates = round_gates.reshape(rounds, groups, GROUP)
    mine = round_gates >= 0.0
    order = jnp.arange(GROUP)
    upto = (order[:, None] <= order[None, :]).astype(jnp.bfloat16)
    ranks = jnp.einsum(
        "rgt,tu->rgu", mine.astype(jnp.bfloat16), upto, preferred_element_type=jnp.float32
    )
    slots = jnp.where(mine, ranks.astype(jnp.int32) - 1, -1)[:, :, None, :]
    round_gates = round_gates[:, :, None, :]

    attended = attend(queries, keys, values)
    projected = jnp.dot(attended, out_proj, preferred_element_type=jnp.float32)
    residual = (hidden_in[0].astype(jnp.float32) + projected).astype(jnp.bfloat16)
    resid_f = residual.astype(jnp.float32)
    normed = (
        resid_f * lax.rsqrt(jnp.mean(resid_f * resid_f, -1, keepdims=True) + 1e-06) * norm_gain
    ).astype(jnp.bfloat16)

    def one_round(inputs):
        part, part_gates, part_slots = inputs
        tokens = lax.all_gather(part, both, axis=0, tiled=True)
        terms = expert_terms(tokens, part_gates, part_slots, expert_weights, down)
        return lax.psum_scatter(terms, both, scatter_dimension=0, tiled=True)

    parts = normed.reshape(rounds, part_rows, D)
    if rounds == 1:
        mixture = one_round((parts[0], round_gates[0], slots[0]))
    else:
        mixture = lax.map(one_round, (parts, round_gates, slots)).reshape(tok_rows, D)
    layer_out = (resid_f + mixture.astype(jnp.float32)).astype(jnp.bfloat16)
    return (residual[None], layer_out[None])


def solution(mesh):
    return jax.shard_map(
        on_device,
        mesh=mesh,
        in_specs=(
            P("exp", "ctx", None),
            P("exp", "ctx", None),
            P("exp", "ctx", None),
            P("exp", "ctx", None),
            P(),
            P(),
            P("exp", "ctx", None),
            P("exp", "ctx", None),
            P(("ctx", "exp"), None, None, None),
        ),
        out_specs=(P("exp", "ctx", None), P("exp", "ctx", None)),
        check_vma=False,
    )
```

```python
import math

import jax
import jax.numpy as jnp
from jax import lax
from jax.experimental import pallas as pl
from jax.experimental.pallas import tpu as pltpu
from jax.sharding import PartitionSpec as P

D = 2048
HEADS = 16
KV_HEADS = 2
HEAD_DIM = 128
TOP = 8
GROUP = 512
ROUND_TOKENS = 8192


def attend(queries, keys, values):
    tok_rows = queries.shape[1]
    group_size = HEADS // KV_HEADS
    score_scale = 1.0 / math.sqrt(HEAD_DIM)
    query_heads = queries[0].reshape(tok_rows, KV_HEADS, group_size, HEAD_DIM)
    first_row = lax.axis_index("ctx") * tok_rows
    query_pos = first_row + jnp.arange(tok_rows, dtype=jnp.int32)
    last_row = first_row + tok_rows - 1
    running = (
        jnp.full((tok_rows, KV_HEADS, group_size), -1e30, jnp.float32),
        jnp.zeros((tok_rows, KV_HEADS, group_size), jnp.float32),
        jnp.zeros((tok_rows, KV_HEADS, group_size, HEAD_DIM), jnp.float32),
    )
    key_piece = lax.all_gather(keys[0], "ctx", axis=0, tiled=True)
    value_piece = lax.all_gather(values[0], "ctx", axis=0, tiled=True)
    piece_rows = key_piece.shape[0]
    absorb_block_rows = math.gcd(piece_rows, 512)

    def one_block(index, running):
        block_start = index * absorb_block_rows

        def compute(running):
            running_max, denom, accum = running
            key_rows = lax.dynamic_slice_in_dim(
                key_piece, block_start, absorb_block_rows, 0
            ).reshape(absorb_block_rows, KV_HEADS, HEAD_DIM)
            value_rows = lax.dynamic_slice_in_dim(
                value_piece, block_start, absorb_block_rows, 0
            ).reshape(absorb_block_rows, KV_HEADS, HEAD_DIM)
            scores = (
                jnp.einsum(
                    "tgjd,ngd->tgjn", query_heads, key_rows, preferred_element_type=jnp.float32
                )
                * score_scale
            )
            key_pos = block_start + jnp.arange(absorb_block_rows, dtype=jnp.int32)
            visible = (key_pos[None, :] <= query_pos[:, None])[:, None, None, :]
            scores = jnp.where(visible, scores, -1e30)
            new_max = jnp.maximum(running_max, scores.max(-1))
            exps = jnp.where(visible, jnp.exp(scores - new_max[..., None]), 0.0)
            rescale = jnp.exp(running_max - new_max)
            denom = denom * rescale + exps.sum(-1)
            added = jnp.einsum(
                "tgjn,ngd->tgjd",
                exps.astype(jnp.bfloat16),
                value_rows,
                preferred_element_type=jnp.float32,
            )
            accum = accum * rescale[..., None] + added
            return (new_max, denom, accum)

        return lax.cond(block_start <= last_row, compute, lambda state: state, running)

    running_max, denom, accum = lax.fori_loop(
        0, piece_rows // absorb_block_rows, one_block, running
    )
    return (accum / denom[..., None]).reshape(tok_rows, HEADS * HEAD_DIM).astype(jnp.bfloat16)


def expert_kernel(gate_ref, slot_ref, tok_ref, weight_ref, down_ref, out_ref):
    slots = slot_ref[0]
    rows = GROUP // 2
    chosen = slots == lax.broadcasted_iota(jnp.int32, (rows, GROUP), 0)
    row_gates = jnp.sum(jnp.where(chosen, gate_ref[0], 0.0), axis=1, keepdims=True)
    pick = chosen.astype(jnp.float32).astype(jnp.bfloat16)
    tokens = jnp.dot(pick, tok_ref[...], preferred_element_type=jnp.float32).astype(jnp.bfloat16)
    gate_part = jnp.dot(tokens, weight_ref[0, 0], preferred_element_type=jnp.float32)
    upper_part = jnp.dot(tokens, weight_ref[0, 1], preferred_element_type=jnp.float32)
    hidden = (gate_part / (1.0 + jnp.exp(-gate_part)) * upper_part).astype(jnp.bfloat16)
    result = jnp.dot(hidden, down_ref[...], preferred_element_type=jnp.float32)
    scaled = (result.astype(jnp.bfloat16).astype(jnp.float32) * row_gates).astype(jnp.bfloat16)
    out_ref[...] = lax.dot_general(
        pick, scaled, (((0,), (0,)), ((), ())), preferred_element_type=jnp.float32
    ).astype(jnp.bfloat16)


def expert_terms(tokens, gates, slots, weights, down):
    groups = tokens.shape[0] // GROUP
    ff = weights.shape[-1]
    return pl.pallas_call(
        expert_kernel,
        grid=(groups,),
        in_specs=[
            pl.BlockSpec((1, 1, GROUP), lambda i: (i, 0, 0)),
            pl.BlockSpec((1, 1, GROUP), lambda i: (i, 0, 0)),
            pl.BlockSpec((GROUP, D), lambda i: (i, 0)),
            pl.BlockSpec((1, 2, D, ff), lambda i: (0, 0, 0, 0)),
            pl.BlockSpec((ff, D), lambda i: (0, 0)),
        ],
        out_specs=pl.BlockSpec((GROUP, D), lambda i: (i, 0)),
        out_shape=jax.ShapeDtypeStruct(tokens.shape, jnp.bfloat16),
        compiler_params=pltpu.CompilerParams(vmem_limit_bytes=56 * 1024 * 1024),
        cost_estimate=pl.CostEstimate(
            flops=tokens.shape[0] * D * (3 * ff + 2 * GROUP),
            bytes_accessed=4 * tokens.size + 6 * D * ff,
            transcendentals=tokens.shape[0] * ff // 2,
        ),
    )(gates, slots, tokens, weights, down)


def scatter_sum_kernel(term_ref, out_ref, held, own, first, second, from_z, load_sem, core_send,
                       core_recv, first_send, first_recv, second_send, second_recv, z_send, z_recv):
    ctx, exp = lax.axis_index("ctx"), lax.axis_index("exp")
    z, core = ctx // 2, ctx % 2
    y, x = exp // 2, exp % 2
    beside_x, beside_y = y * 2 + (1 - x), (1 - y) * 2 + x
    owners = (exp, beside_x, beside_y, (1 - y) * 2 + (1 - x))
    sibling = (z * 2 + (1 - core), exp)
    plane_peer = ((ctx, beside_x), (ctx, beside_y))
    z_of = [(z + 1 + k) % 4 for k in range(4)]
    z_peer = [(z_of[k] * 2 + core, exp) for k in range(3)]
    rows, width = out_ref.shape
    half = width // 2
    columns = (pl.ds(0, half), pl.ds(half, half))
    piece = min(rows, 32)

    def remote(source, target, send, recv, device):
        return pltpu.make_async_remote_copy(
            src_ref=source, dst_ref=target, send_sem=send, recv_sem=recv,
            device_id=device, device_id_type=pl.DeviceIdType.MESH,
        )

    def add_rows(target, one, other):
        def some(i, carry):
            part = pl.ds(pl.multiple_of(i * piece, piece), piece)
            target[part, :] = one[part, :] + other[part, :]
            return carry

        lax.fori_loop(0, rows // piece, some, 0)

    barrier = pltpu.get_barrier_semaphore()
    partners = (sibling,) + plane_peer + tuple(z_peer)
    for device in partners:
        pl.semaphore_signal(barrier, inc=1, device_id=device, device_id_type=pl.DeviceIdType.MESH)
    pl.semaphore_wait(barrier, len(partners))

    loads, core_copies, first_copies, second_copies, z_copies = {}, {}, {}, {}, {}
    for k in range(4):
        for r in (3, 1, 2, 0):
            slot = k * 4 + r
            block = (z_of[k] * 2) * 4 + owners[r]
            core_copies[slot] = remote(
                term_ref.at[block + (1 - core) * 4], held.at[slot],
                core_send.at[slot], core_recv.at[slot], sibling,
            )
            core_copies[slot].start()
            loads[slot] = pltpu.make_async_copy(
                term_ref.at[block + core * 4], own.at[slot], load_sem.at[slot]
            )
            loads[slot].start()

    def send_first(k, h, j, r):
        index = k * 4 + h * 2 + j
        first_copies[index] = remote(
            held.at[k * 4 + r, :, columns[h]], first.at[index],
            first_send.at[index], first_recv.at[index], plane_peer[h],
        )
        first_copies[index].start()

    def over_core(k):
        for r in (3, 1, 2, 0):
            slot = k * 4 + r
            core_copies[slot].wait_recv()
            loads[slot].wait()
            add_rows(held.at[slot], held.at[slot], own.at[slot])
            if r == 3:
                send_first(k, 0, 1, 3)
                send_first(k, 1, 1, 3)
            elif r == 1:
                send_first(k, 0, 0, 1)
            elif r == 2:
                send_first(k, 1, 0, 2)

    def over_first(k):
        for h in range(2):
            index = k * 4 + h * 2 + 1
            first_copies[index].wait_recv()
            mine = held.at[k * 4 + 2 - h, :, columns[h]]
            add_rows(first.at[index], first.at[index], mine)
            place = k * 2 + h
            second_copies[place] = remote(
                first.at[index], second.at[place],
                second_send.at[place], second_recv.at[place], plane_peer[1 - h],
            )
            second_copies[place].start()
        for h in range(2):
            index = k * 4 + h * 2
            first_copies[index].wait_recv()
            add_rows(first.at[index], first.at[index], held.at[k * 4, :, columns[h]])

    def over_second(k):
        for h in range(2):
            second_copies[k * 2 + h].wait_recv()
            total = own.at[k * 4, :, columns[h]]
            add_rows(total, first.at[k * 4 + h * 2], second.at[k * 2 + h])
        if k < 3:
            z_copies[k] = remote(
                own.at[k * 4], from_z.at[k], z_send.at[k], z_recv.at[k], z_peer[k]
            )
            z_copies[k].start()

    for step in range(6):
        if step < 4:
            over_core(step)
        if 1 <= step < 5:
            over_first(step - 1)
        if step >= 2:
            over_second(step - 2)

    for k in range(3):
        z_copies[k].wait_recv()

    def finish(i, carry):
        part = pl.ds(pl.multiple_of(i * piece, piece), piece)
        total = own[12, part, :].astype(jnp.float32)
        for k in range(3):
            total += from_z[k, part, :].astype(jnp.float32)
        out_ref[part, :] = total.astype(jnp.bfloat16)
        return carry

    lax.fori_loop(0, rows // piece, finish, 0)
    for copies in (core_copies, first_copies, second_copies, z_copies):
        for copy in copies.values():
            copy.wait_send()


def scatter_sum(terms, n_ctx, n_exp):
    if (n_ctx, n_exp) != (8, 4):
        return lax.psum_scatter(terms, ("ctx", "exp"), scatter_dimension=0, tiled=True)
    rows, width = terms.shape[0] // 32, terms.shape[1]
    return pl.pallas_call(
        scatter_sum_kernel,
        out_shape=jax.ShapeDtypeStruct((rows, width), jnp.bfloat16),
        in_specs=[pl.BlockSpec(memory_space=pl.ANY)],
        out_specs=pl.BlockSpec(memory_space=pltpu.VMEM),
        scratch_shapes=[
            pltpu.VMEM((16, rows, width), jnp.bfloat16),
            pltpu.VMEM((16, rows, width), jnp.bfloat16),
            pltpu.VMEM((16, rows, width // 2), jnp.bfloat16),
            pltpu.VMEM((8, rows, width // 2), jnp.bfloat16),
            pltpu.VMEM((3, rows, width), jnp.bfloat16),
        ]
        + [pltpu.SemaphoreType.DMA((n,)) for n in (16, 16, 16, 16, 16, 8, 8, 3, 3)],
        compiler_params=pltpu.CompilerParams(
            collective_id=0, has_side_effects=True, vmem_limit_bytes=58 * 1024 * 1024
        ),
        cost_estimate=pl.CostEstimate(
            flops=2 * terms.size, bytes_accessed=2 * terms.size, transcendentals=0
        ),
    )(terms.reshape(32, rows, width))


def on_device(
    queries, keys, values, hidden_in, out_proj, norm_gain, route_ids, route_scores, expert_weights
):
    tok_rows = queries.shape[1]
    both = ("ctx", "exp")
    n_dev = lax.axis_size("ctx") * lax.axis_size("exp")
    gates = jax.nn.softmax(route_scores[0], -1)
    named = route_ids[0][None, :, :] == jnp.arange(n_dev, dtype=jnp.int32)[:, None, None]
    by_expert = jnp.sum(jnp.where(named, gates[None], 0.0), -1)
    by_expert = jnp.where(jnp.any(named, -1), by_expert, -1.0)
    my_gates = lax.all_to_all(by_expert, both, split_axis=0, concat_axis=0, tiled=True)
    down = expert_weights[0, 2].T

    rounds = n_dev * tok_rows // ROUND_TOKENS
    part_rows = tok_rows // rounds
    groups = ROUND_TOKENS // GROUP
    round_gates = my_gates.reshape(n_dev, rounds, part_rows).transpose(1, 0, 2)
    round_gates = round_gates.reshape(rounds, groups, GROUP)
    mine = round_gates >= 0.0
    order = jnp.arange(GROUP)
    upto = (order[:, None] <= order[None, :]).astype(jnp.bfloat16)
    ranks = jnp.einsum(
        "rgt,tu->rgu", mine.astype(jnp.bfloat16), upto, preferred_element_type=jnp.float32
    )
    slots = jnp.where(mine, ranks.astype(jnp.int32) - 1, -1)[:, :, None, :]
    round_gates = round_gates[:, :, None, :]

    attended = attend(queries, keys, values)
    projected = jnp.dot(attended, out_proj, preferred_element_type=jnp.float32)
    residual = (hidden_in[0].astype(jnp.float32) + projected).astype(jnp.bfloat16)
    resid_f = residual.astype(jnp.float32)
    normed = (
        resid_f * lax.rsqrt(jnp.mean(resid_f * resid_f, -1, keepdims=True) + 1e-06) * norm_gain
    ).astype(jnp.bfloat16)

    def one_round(inputs):
        part, part_gates, part_slots = inputs
        tokens = lax.all_gather(part, both, axis=0, tiled=True)
        terms = expert_terms(tokens, part_gates, part_slots, expert_weights, down)
        return scatter_sum(terms, lax.axis_size("ctx"), lax.axis_size("exp"))

    parts = normed.reshape(rounds, part_rows, D)
    if rounds == 1:
        mixture = one_round((parts[0], round_gates[0], slots[0]))
    else:
        mixture = lax.map(one_round, (parts, round_gates, slots)).reshape(tok_rows, D)
    layer_out = (resid_f + mixture.astype(jnp.float32)).astype(jnp.bfloat16)
    return (residual[None], layer_out[None])


def solution(mesh):
    return jax.shard_map(
        on_device,
        mesh=mesh,
        in_specs=(
            P("exp", "ctx", None),
            P("exp", "ctx", None),
            P("exp", "ctx", None),
            P("exp", "ctx", None),
            P(),
            P(),
            P("exp", "ctx", None),
            P("exp", "ctx", None),
            P(("ctx", "exp"), None, None, None),
        ),
        out_specs=(P("exp", "ctx", None), P("exp", "ctx", None)),
        check_vma=False,
    )
```

```python
import math

import jax
import jax.numpy as jnp
from jax import lax
from jax.experimental import pallas as pl
from jax.experimental.pallas import tpu as pltpu
from jax.sharding import PartitionSpec as P

D = 2048
HEADS = 16
KV_HEADS = 2
HEAD_DIM = 128
TOP = 8
GROUP = 512
ROUND_TOKENS = 8192


def attend(queries, keys, values):
    tok_rows = queries.shape[1]
    group_size = HEADS // KV_HEADS
    score_scale = 1.0 / math.sqrt(HEAD_DIM)
    query_heads = queries[0].reshape(tok_rows, KV_HEADS, group_size, HEAD_DIM)
    first_row = lax.axis_index("ctx") * tok_rows
    query_pos = first_row + jnp.arange(tok_rows, dtype=jnp.int32)
    last_row = first_row + tok_rows - 1
    running = (
        jnp.full((tok_rows, KV_HEADS, group_size), -1e30, jnp.float32),
        jnp.zeros((tok_rows, KV_HEADS, group_size), jnp.float32),
        jnp.zeros((tok_rows, KV_HEADS, group_size, HEAD_DIM), jnp.float32),
    )
    both_rows = jnp.concatenate([keys[0], values[0]], axis=1)
    both_piece = lax.all_gather(both_rows, "ctx", axis=0, tiled=True)
    key_piece, value_piece = jnp.split(both_piece, 2, axis=1)
    piece_rows = key_piece.shape[0]
    absorb_block_rows = math.gcd(piece_rows, 512)

    def one_block(index, running):
        block_start = index * absorb_block_rows

        def compute(running):
            running_max, denom, accum = running
            key_rows = lax.dynamic_slice_in_dim(
                key_piece, block_start, absorb_block_rows, 0
            ).reshape(absorb_block_rows, KV_HEADS, HEAD_DIM)
            value_rows = lax.dynamic_slice_in_dim(
                value_piece, block_start, absorb_block_rows, 0
            ).reshape(absorb_block_rows, KV_HEADS, HEAD_DIM)
            scores = (
                jnp.einsum(
                    "tgjd,ngd->tgjn", query_heads, key_rows, preferred_element_type=jnp.float32
                )
                * score_scale
            )
            key_pos = block_start + jnp.arange(absorb_block_rows, dtype=jnp.int32)
            visible = (key_pos[None, :] <= query_pos[:, None])[:, None, None, :]
            scores = jnp.where(visible, scores, -1e30)
            new_max = jnp.maximum(running_max, scores.max(-1))
            exps = jnp.where(visible, jnp.exp(scores - new_max[..., None]), 0.0)
            rescale = jnp.exp(running_max - new_max)
            denom = denom * rescale + exps.sum(-1)
            added = jnp.einsum(
                "tgjn,ngd->tgjd",
                exps.astype(jnp.bfloat16),
                value_rows,
                preferred_element_type=jnp.float32,
            )
            accum = accum * rescale[..., None] + added
            return (new_max, denom, accum)

        return lax.cond(block_start <= last_row, compute, lambda state: state, running)

    running_max, denom, accum = lax.fori_loop(
        0, piece_rows // absorb_block_rows, one_block, running
    )
    return (accum / denom[..., None]).reshape(tok_rows, HEADS * HEAD_DIM).astype(jnp.bfloat16)


def expert_kernel(gate_ref, slot_ref, tok_ref, weight_ref, down_ref, out_ref):
    slots = slot_ref[0]
    rows = GROUP // 2
    chosen = slots == lax.broadcasted_iota(jnp.int32, (rows, GROUP), 0)
    row_gates = jnp.sum(jnp.where(chosen, gate_ref[0], 0.0), axis=1, keepdims=True)
    pick = chosen.astype(jnp.float32).astype(jnp.bfloat16)
    tokens = jnp.dot(pick, tok_ref[...], preferred_element_type=jnp.float32).astype(jnp.bfloat16)
    gate_part = jnp.dot(tokens, weight_ref[0, 0], preferred_element_type=jnp.float32)
    upper_part = jnp.dot(tokens, weight_ref[0, 1], preferred_element_type=jnp.float32)
    hidden = (gate_part / (1.0 + jnp.exp(-gate_part)) * upper_part).astype(jnp.bfloat16)
    result = jnp.dot(hidden, down_ref[...], preferred_element_type=jnp.float32)
    scaled = (result.astype(jnp.bfloat16).astype(jnp.float32) * row_gates).astype(jnp.bfloat16)
    out_ref[...] = lax.dot_general(
        pick, scaled, (((0,), (0,)), ((), ())), preferred_element_type=jnp.float32
    ).astype(jnp.bfloat16)


def expert_terms(tokens, gates, slots, weights, down):
    groups = tokens.shape[0] // GROUP
    ff = weights.shape[-1]
    return pl.pallas_call(
        expert_kernel,
        grid=(groups,),
        in_specs=[
            pl.BlockSpec((1, 1, GROUP), lambda i: (i, 0, 0)),
            pl.BlockSpec((1, 1, GROUP), lambda i: (i, 0, 0)),
            pl.BlockSpec((GROUP, D), lambda i: (i, 0)),
            pl.BlockSpec((1, 2, D, ff), lambda i: (0, 0, 0, 0)),
            pl.BlockSpec((ff, D), lambda i: (0, 0)),
        ],
        out_specs=pl.BlockSpec((GROUP, D), lambda i: (i, 0)),
        out_shape=jax.ShapeDtypeStruct(tokens.shape, jnp.bfloat16),
        compiler_params=pltpu.CompilerParams(vmem_limit_bytes=56 * 1024 * 1024),
        cost_estimate=pl.CostEstimate(
            flops=tokens.shape[0] * D * (3 * ff + 2 * GROUP),
            bytes_accessed=4 * tokens.size + 6 * D * ff,
            transcendentals=tokens.shape[0] * ff // 2,
        ),
    )(gates, slots, tokens, weights, down)


def scatter_sum_kernel(term_ref, out_ref, held, own, first, second, from_z, load_sem, core_send,
                       core_recv, first_send, first_recv, second_send, second_recv, z_send, z_recv):
    ctx, exp = lax.axis_index("ctx"), lax.axis_index("exp")
    z, core = ctx // 2, ctx % 2
    y, x = exp // 2, exp % 2
    beside_x, beside_y = y * 2 + (1 - x), (1 - y) * 2 + x
    owners = (exp, beside_x, beside_y, (1 - y) * 2 + (1 - x))
    sibling = (z * 2 + (1 - core), exp)
    plane_peer = ((ctx, beside_x), (ctx, beside_y))
    z_of = [(z + 1 + k) % 4 for k in range(4)]
    z_peer = [(z_of[k] * 2 + core, exp) for k in range(3)]
    rows, width = out_ref.shape
    half = width // 2
    columns = (pl.ds(0, half), pl.ds(half, half))
    piece = min(rows, 32)

    def remote(source, target, send, recv, device):
        return pltpu.make_async_remote_copy(
            src_ref=source, dst_ref=target, send_sem=send, recv_sem=recv,
            device_id=device, device_id_type=pl.DeviceIdType.MESH,
        )

    def add_rows(target, one, other):
        def some(i, carry):
            part = pl.ds(pl.multiple_of(i * piece, piece), piece)
            target[part, :] = one[part, :] + other[part, :]
            return carry

        lax.fori_loop(0, rows // piece, some, 0)

    barrier = pltpu.get_barrier_semaphore()
    partners = (sibling,) + plane_peer + tuple(z_peer)
    for device in partners:
        pl.semaphore_signal(barrier, inc=1, device_id=device, device_id_type=pl.DeviceIdType.MESH)
    pl.semaphore_wait(barrier, len(partners))

    loads, core_copies, first_copies, second_copies, z_copies = {}, {}, {}, {}, {}
    for k in range(4):
        for r in (3, 1, 2, 0):
            slot = k * 4 + r
            block = (z_of[k] * 2) * 4 + owners[r]
            core_copies[slot] = remote(
                term_ref.at[block + (1 - core) * 4], held.at[slot],
                core_send.at[slot], core_recv.at[slot], sibling,
            )
            core_copies[slot].start()
            loads[slot] = pltpu.make_async_copy(
                term_ref.at[block + core * 4], own.at[slot], load_sem.at[slot]
            )
            loads[slot].start()

    def send_first(k, h, j, r):
        index = k * 4 + h * 2 + j
        first_copies[index] = remote(
            held.at[k * 4 + r, :, columns[h]], first.at[index],
            first_send.at[index], first_recv.at[index], plane_peer[h],
        )
        first_copies[index].start()

    def over_core(k):
        for r in (3, 1, 2, 0):
            slot = k * 4 + r
            core_copies[slot].wait_recv()
            loads[slot].wait()
            add_rows(held.at[slot], held.at[slot], own.at[slot])
            if r == 3:
                send_first(k, 0, 1, 3)
                send_first(k, 1, 1, 3)
            elif r == 1:
                send_first(k, 0, 0, 1)
            elif r == 2:
                send_first(k, 1, 0, 2)

    def over_first(k):
        for h in range(2):
            index = k * 4 + h * 2 + 1
            first_copies[index].wait_recv()
            mine = held.at[k * 4 + 2 - h, :, columns[h]]
            add_rows(first.at[index], first.at[index], mine)
            place = k * 2 + h
            second_copies[place] = remote(
                first.at[index], second.at[place],
                second_send.at[place], second_recv.at[place], plane_peer[1 - h],
            )
            second_copies[place].start()
        for h in range(2):
            index = k * 4 + h * 2
            first_copies[index].wait_recv()
            add_rows(first.at[index], first.at[index], held.at[k * 4, :, columns[h]])

    def over_second(k):
        for h in range(2):
            second_copies[k * 2 + h].wait_recv()
            total = own.at[k * 4, :, columns[h]]
            add_rows(total, first.at[k * 4 + h * 2], second.at[k * 2 + h])
        if k < 3:
            z_copies[k] = remote(
                own.at[k * 4], from_z.at[k], z_send.at[k], z_recv.at[k], z_peer[k]
            )
            z_copies[k].start()

    for step in range(6):
        if step < 4:
            over_core(step)
        if 1 <= step < 5:
            over_first(step - 1)
        if step >= 2:
            over_second(step - 2)

    for k in range(3):
        z_copies[k].wait_recv()

    def finish(i, carry):
        part = pl.ds(pl.multiple_of(i * piece, piece), piece)
        total = own[12, part, :].astype(jnp.float32)
        for k in range(3):
            total += from_z[k, part, :].astype(jnp.float32)
        out_ref[part, :] = total.astype(jnp.bfloat16)
        return carry

    lax.fori_loop(0, rows // piece, finish, 0)
    for copies in (core_copies, first_copies, second_copies, z_copies):
        for copy in copies.values():
            copy.wait_send()


def scatter_sum(terms):
    rows, width = terms.shape[1:]
    return pl.pallas_call(
        scatter_sum_kernel,
        out_shape=jax.ShapeDtypeStruct((rows, width), jnp.bfloat16),
        in_specs=[pl.BlockSpec(memory_space=pl.ANY)],
        out_specs=pl.BlockSpec(memory_space=pltpu.VMEM),
        scratch_shapes=[
            pltpu.VMEM((16, rows, width), jnp.bfloat16),
            pltpu.VMEM((16, rows, width), jnp.bfloat16),
            pltpu.VMEM((16, rows, width // 2), jnp.bfloat16),
            pltpu.VMEM((8, rows, width // 2), jnp.bfloat16),
            pltpu.VMEM((3, rows, width), jnp.bfloat16),
        ]
        + [pltpu.SemaphoreType.DMA((n,)) for n in (16, 16, 16, 16, 16, 8, 8, 3, 3)],
        compiler_params=pltpu.CompilerParams(
            collective_id=0, has_side_effects=True, vmem_limit_bytes=58 * 1024 * 1024
        ),
        cost_estimate=pl.CostEstimate(
            flops=2 * terms.size, bytes_accessed=2 * terms.size, transcendentals=0
        ),
    )(terms)


def gather_expert_kernel(tok_ref, gate_ref, slot_ref, weight_ref, down_ref, term_ref,
                         held, upper, down, picked, out, own_sem, weight_sem, out_sem,
                         z_send, z_recv, side_send, side_recv, diag_send, diag_recv,
                         core_send, core_recv):
    ctx, exp = lax.axis_index("ctx"), lax.axis_index("exp")
    z, core = ctx // 2, ctx % 2
    y, x = exp // 2, exp % 2
    beside_x, beside_y = y * 2 + (1 - x), (1 - y) * 2 + x
    owners = (exp, beside_x, beside_y, (1 - y) * 2 + (1 - x))
    sibling = (z * 2 + (1 - core), exp)
    plane_peer = ((ctx, beside_x), (ctx, beside_y))
    z_peer = [(((z + k) % 4) * 2 + core, exp) for k in (1, 2, 3)]
    rows, width = tok_ref.shape
    chunk = min(width, 512)
    mine = pl.ds(pl.multiple_of(core * rows, rows), rows)
    theirs = pl.ds(pl.multiple_of((1 - core) * rows, rows), rows)

    def remote(source, target, send, recv, device):
        return pltpu.make_async_remote_copy(
            src_ref=source, dst_ref=target, send_sem=send, recv_sem=recv,
            device_id=device, device_id_type=pl.DeviceIdType.MESH,
        )

    def z_copy(k):
        return remote(tok_ref, held.at[k * 4, mine], z_send.at[k - 1], z_recv.at[k - 1],
                      z_peer[k - 1])

    def z_arrival(k):
        return remote(tok_ref, held.at[k * 4, mine], z_send.at[k - 1], z_recv.at[k - 1],
                      z_peer[0])

    def side_copy(k, h):
        return remote(held.at[k * 4, mine], held.at[k * 4 + 1 + h, mine],
                      side_send.at[k * 2 + h], side_recv.at[k * 2 + h], plane_peer[h])

    def diag_copy(k, h):
        half = pl.ds(pl.multiple_of(core * rows + h * (rows // 2), rows // 2), rows // 2)
        return remote(held.at[k * 4 + 2 - h, half], held.at[k * 4 + 3, half],
                      diag_send.at[k * 2 + h], diag_recv.at[k * 2 + h], plane_peer[h])

    def core_copy(k, r):
        slot = k * 4 + r
        return remote(held.at[slot, mine], held.at[slot, mine],
                      core_send.at[slot], core_recv.at[slot], sibling)

    def core_arrival(k, r):
        slot = k * 4 + r
        return remote(held.at[slot, theirs], held.at[slot, theirs],
                      core_send.at[slot], core_recv.at[slot], sibling)

    def out_copy(k, r, c):
        block = (((z - k + 4) % 4) * 2 + c) * 4 + owners[r]
        return pltpu.make_async_copy(
            out.at[r % 2, pl.ds(c * rows, rows)], term_ref.at[block], out_sem.at[r % 2, c]
        )

    upper_load = pltpu.make_async_copy(weight_ref.at[0, pl.ds(0, 2)], upper, weight_sem.at[0])
    down_load = pltpu.make_async_copy(down_ref, down, weight_sem.at[1])
    own_load = pltpu.make_async_copy(tok_ref, held.at[0, mine], own_sem)
    own_load.start()
    upper_load.start()
    down_load.start()

    barrier = pltpu.get_barrier_semaphore()
    partners = (sibling,) + plane_peer + tuple(z_peer)
    for device in partners:
        pl.semaphore_signal(barrier, inc=1, device_id=device, device_id_type=pl.DeviceIdType.MESH)
    pl.semaphore_wait(barrier, len(partners))

    def spread(k):
        side_copy(k, 0).start()
        side_copy(k, 1).start()
        core_copy(k, 0).start()

    own_load.wait()
    spread(0)
    for k in (1, 2, 3):
        z_copy(k).start()
    upper_load.wait()
    down_load.wait()

    def serve(k, r):
        slot = k * 4 + r
        core_arrival(k, r).wait_recv()
        if r >= 2:
            for c in range(2):
                out_copy(k, r - 2, c).wait()
        else:
            @pl.when(k > 0)
            def _():
                for c in range(2):
                    out_copy(k - 1, r + 2, c).wait()

        group = ((z - k + 4) % 4) * 4 + owners[r]
        chosen = slot_ref[group] == lax.broadcasted_iota(jnp.int32, (rows, 2 * rows), 0)
        row_gates = jnp.sum(jnp.where(chosen, gate_ref[group], 0.0), axis=1, keepdims=True)
        pick = chosen.astype(jnp.float32).astype(jnp.bfloat16)

        def take(i, carry):
            part = pl.ds(pl.multiple_of(i * chunk, chunk), chunk)
            picked[:, part] = jnp.dot(
                pick, held[slot, :, part], preferred_element_type=jnp.float32
            ).astype(jnp.bfloat16)
            return carry

        lax.fori_loop(0, width // chunk, take, 0)
        gate_part = jnp.dot(picked[...], upper[0], preferred_element_type=jnp.float32)
        upper_part = jnp.dot(picked[...], upper[1], preferred_element_type=jnp.float32)
        hidden = (gate_part / (1.0 + jnp.exp(-gate_part)) * upper_part).astype(jnp.bfloat16)

        def give(i, carry):
            part = pl.ds(pl.multiple_of(i * chunk, chunk), chunk)
            result = jnp.dot(hidden, down[:, part], preferred_element_type=jnp.float32)
            scaled = result.astype(jnp.bfloat16).astype(jnp.float32) * row_gates
            out[r % 2, :, part] = lax.dot_general(
                pick, scaled.astype(jnp.bfloat16), (((0,), (0,)), ((), ())),
                preferred_element_type=jnp.float32,
            ).astype(jnp.bfloat16)
            return carry

        lax.fori_loop(0, width // chunk, give, 0)
        for c in range(2):
            out_copy(k, r, c).start()

    def step(k, carry):
        serve(k, 0)
        side_copy(k, 0).wait_recv()
        diag_copy(k, 1).start()
        core_copy(k, 1).start()
        side_copy(k, 1).wait_recv()
        diag_copy(k, 0).start()
        core_copy(k, 2).start()
        serve(k, 1)

        @pl.when(k < 3)
        def _():
            z_arrival(k + 1).wait_recv()
            spread(k + 1)

        serve(k, 2)
        diag_copy(k, 0).wait_recv()
        diag_copy(k, 1).wait_recv()
        core_copy(k, 3).start()
        serve(k, 3)
        return carry

    lax.fori_loop(0, 4, step, 0)
    for r in (2, 3):
        for c in range(2):
            out_copy(3, r, c).wait()
    for k in (1, 2, 3):
        z_copy(k).wait_send()

    def drain(k, carry):
        for h in range(2):
            side_copy(k, h).wait_send()
            diag_copy(k, h).wait_send()
        for r in range(4):
            core_copy(k, r).wait_send()
        return carry

    lax.fori_loop(0, 4, drain, 0)


def gathered_terms(tokens, gates, slots, weights, down):
    rows, width = tokens.shape
    ff = weights.shape[-1]
    vmem = pl.BlockSpec(memory_space=pltpu.VMEM)
    hbm = pl.BlockSpec(memory_space=pl.ANY)
    return pl.pallas_call(
        gather_expert_kernel,
        out_shape=jax.ShapeDtypeStruct((32, rows, width), jnp.bfloat16),
        in_specs=[vmem, vmem, vmem, hbm, hbm],
        out_specs=hbm,
        scratch_shapes=[
            pltpu.VMEM((16, 2 * rows, width), jnp.bfloat16),
            pltpu.VMEM((2, width, ff), jnp.bfloat16),
            pltpu.VMEM((ff, width), jnp.bfloat16),
            pltpu.VMEM((rows, width), jnp.bfloat16),
            pltpu.VMEM((2, 2 * rows, width), jnp.bfloat16),
            pltpu.SemaphoreType.DMA,
            pltpu.SemaphoreType.DMA((2,)),
            pltpu.SemaphoreType.DMA((2, 2)),
        ]
        + [pltpu.SemaphoreType.DMA((n,)) for n in (3, 3, 8, 8, 8, 8, 16, 16)],
        compiler_params=pltpu.CompilerParams(
            collective_id=1, has_side_effects=True, vmem_limit_bytes=58 * 1024 * 1024
        ),
        cost_estimate=pl.CostEstimate(
            flops=32 * rows * width * (3 * ff + 4 * rows),
            bytes_accessed=64 * rows * width + 6 * width * ff,
            transcendentals=16 * rows * ff,
        ),
    )(tokens, gates, slots, weights, down)


def on_device(
    queries, keys, values, hidden_in, out_proj, norm_gain, route_ids, route_scores, expert_weights
):
    tok_rows = queries.shape[1]
    both = ("ctx", "exp")
    n_dev = lax.axis_size("ctx") * lax.axis_size("exp")
    gates = jax.nn.softmax(route_scores[0], -1)
    named = route_ids[0][None, :, :] == jnp.arange(n_dev, dtype=jnp.int32)[:, None, None]
    by_expert = jnp.sum(jnp.where(named, gates[None], 0.0), -1)
    by_expert = jnp.where(jnp.any(named, -1), by_expert, -1.0)
    my_gates = lax.all_to_all(by_expert, both, split_axis=0, concat_axis=0, tiled=True)
    down = expert_weights[0, 2].T

    kernel_mesh = (lax.axis_size("ctx"), lax.axis_size("exp")) == (8, 4)
    rounds = n_dev * tok_rows // ROUND_TOKENS
    part_rows = tok_rows // rounds
    groups = ROUND_TOKENS // GROUP
    if kernel_mesh:
        round_gates = my_gates.reshape(4, 2, 4, tok_rows).transpose(0, 2, 1, 3)
    else:
        round_gates = my_gates.reshape(n_dev, rounds, part_rows).transpose(1, 0, 2)
    round_gates = round_gates.reshape(rounds, groups, GROUP)
    mine = round_gates >= 0.0
    order = jnp.arange(GROUP)
    upto = (order[:, None] <= order[None, :]).astype(jnp.bfloat16)
    ranks = jnp.einsum(
        "rgt,tu->rgu", mine.astype(jnp.bfloat16), upto, preferred_element_type=jnp.float32
    )
    slots = jnp.where(mine, ranks.astype(jnp.int32) - 1, -1)[:, :, None, :]
    round_gates = round_gates[:, :, None, :]

    attended = attend(queries, keys, values)
    projected = jnp.dot(attended, out_proj, preferred_element_type=jnp.float32)
    residual = (hidden_in[0].astype(jnp.float32) + projected).astype(jnp.bfloat16)
    resid_f = residual.astype(jnp.float32)
    normed = (
        resid_f * lax.rsqrt(jnp.mean(resid_f * resid_f, -1, keepdims=True) + 1e-06) * norm_gain
    ).astype(jnp.bfloat16)

    def one_round(inputs):
        part, part_gates, part_slots = inputs
        tokens = lax.all_gather(part, both, axis=0, tiled=True)
        terms = expert_terms(tokens, part_gates, part_slots, expert_weights, down)
        return lax.psum_scatter(terms, both, scatter_dimension=0, tiled=True)

    parts = normed.reshape(rounds, part_rows, D)
    if kernel_mesh:
        terms = gathered_terms(normed, round_gates[0], slots[0], expert_weights, down)
        mixture = scatter_sum(terms)
    elif rounds == 1:
        mixture = one_round((parts[0], round_gates[0], slots[0]))
    else:
        mixture = lax.map(one_round, (parts, round_gates, slots)).reshape(tok_rows, D)
    layer_out = (resid_f + mixture.astype(jnp.float32)).astype(jnp.bfloat16)
    return (residual[None], layer_out[None])


def solution(mesh):
    return jax.shard_map(
        on_device,
        mesh=mesh,
        in_specs=(
            P("exp", "ctx", None),
            P("exp", "ctx", None),
            P("exp", "ctx", None),
            P("exp", "ctx", None),
            P(),
            P(),
            P("exp", "ctx", None),
            P("exp", "ctx", None),
            P(("ctx", "exp"), None, None, None),
        ),
        out_specs=(P("exp", "ctx", None), P("exp", "ctx", None)),
        check_vma=False,
    )
```

```python
import math

import jax
import jax.numpy as jnp
from jax import lax
from jax.experimental import pallas as pl
from jax.experimental.pallas import tpu as pltpu
from jax.sharding import PartitionSpec as P

D = 2048
HEADS = 16
KV_HEADS = 2
HEAD_DIM = 128
TOP = 8
GROUP = 512
ROUND_TOKENS = 8192


def attend(queries, keys, values):
    tok_rows = queries.shape[1]
    group_size = HEADS // KV_HEADS
    score_scale = 1.0 / math.sqrt(HEAD_DIM)
    query_heads = queries[0].reshape(tok_rows, KV_HEADS, group_size, HEAD_DIM)
    first_row = lax.axis_index("ctx") * tok_rows
    query_pos = first_row + jnp.arange(tok_rows, dtype=jnp.int32)
    last_row = first_row + tok_rows - 1
    running = (
        jnp.full((tok_rows, KV_HEADS, group_size), -1e30, jnp.float32),
        jnp.zeros((tok_rows, KV_HEADS, group_size), jnp.float32),
        jnp.zeros((tok_rows, KV_HEADS, group_size, HEAD_DIM), jnp.float32),
    )
    both_rows = jnp.concatenate([keys[0], values[0]], axis=1)
    both_piece = lax.all_gather(both_rows, "ctx", axis=0, tiled=True)
    key_piece, value_piece = jnp.split(both_piece, 2, axis=1)
    piece_rows = key_piece.shape[0]
    absorb_block_rows = math.gcd(piece_rows, 512)

    def one_block(index, running):
        block_start = index * absorb_block_rows

        def compute(running):
            running_max, denom, accum = running
            key_rows = lax.dynamic_slice_in_dim(
                key_piece, block_start, absorb_block_rows, 0
            ).reshape(absorb_block_rows, KV_HEADS, HEAD_DIM)
            value_rows = lax.dynamic_slice_in_dim(
                value_piece, block_start, absorb_block_rows, 0
            ).reshape(absorb_block_rows, KV_HEADS, HEAD_DIM)
            scores = (
                jnp.einsum(
                    "tgjd,ngd->tgjn", query_heads, key_rows, preferred_element_type=jnp.float32
                )
                * score_scale
            )
            key_pos = block_start + jnp.arange(absorb_block_rows, dtype=jnp.int32)
            visible = (key_pos[None, :] <= query_pos[:, None])[:, None, None, :]
            scores = jnp.where(visible, scores, -1e30)
            new_max = jnp.maximum(running_max, scores.max(-1))
            exps = jnp.where(visible, jnp.exp(scores - new_max[..., None]), 0.0)
            rescale = jnp.exp(running_max - new_max)
            denom = denom * rescale + exps.sum(-1)
            added = jnp.einsum(
                "tgjn,ngd->tgjd",
                exps.astype(jnp.bfloat16),
                value_rows,
                preferred_element_type=jnp.float32,
            )
            accum = accum * rescale[..., None] + added
            return (new_max, denom, accum)

        return lax.cond(block_start <= last_row, compute, lambda state: state, running)

    running_max, denom, accum = lax.fori_loop(
        0, piece_rows // absorb_block_rows, one_block, running
    )
    return (accum / denom[..., None]).reshape(tok_rows, HEADS * HEAD_DIM).astype(jnp.bfloat16)


def expert_kernel(gate_ref, slot_ref, tok_ref, weight_ref, down_ref, out_ref):
    slots = slot_ref[0]
    rows = GROUP // 2
    chosen = slots == lax.broadcasted_iota(jnp.int32, (rows, GROUP), 0)
    row_gates = jnp.sum(jnp.where(chosen, gate_ref[0], 0.0), axis=1, keepdims=True)
    pick = chosen.astype(jnp.float32).astype(jnp.bfloat16)
    tokens = jnp.dot(pick, tok_ref[...], preferred_element_type=jnp.float32).astype(jnp.bfloat16)
    gate_part = jnp.dot(tokens, weight_ref[0, 0], preferred_element_type=jnp.float32)
    upper_part = jnp.dot(tokens, weight_ref[0, 1], preferred_element_type=jnp.float32)
    hidden = (gate_part / (1.0 + jnp.exp(-gate_part)) * upper_part).astype(jnp.bfloat16)
    result = jnp.dot(hidden, down_ref[...], preferred_element_type=jnp.float32)
    scaled = (result.astype(jnp.bfloat16).astype(jnp.float32) * row_gates).astype(jnp.bfloat16)
    out_ref[...] = lax.dot_general(
        pick, scaled, (((0,), (0,)), ((), ())), preferred_element_type=jnp.float32
    ).astype(jnp.bfloat16)


def expert_terms(tokens, gates, slots, weights, down):
    groups = tokens.shape[0] // GROUP
    ff = weights.shape[-1]
    return pl.pallas_call(
        expert_kernel,
        grid=(groups,),
        in_specs=[
            pl.BlockSpec((1, 1, GROUP), lambda i: (i, 0, 0)),
            pl.BlockSpec((1, 1, GROUP), lambda i: (i, 0, 0)),
            pl.BlockSpec((GROUP, D), lambda i: (i, 0)),
            pl.BlockSpec((1, 2, D, ff), lambda i: (0, 0, 0, 0)),
            pl.BlockSpec((ff, D), lambda i: (0, 0)),
        ],
        out_specs=pl.BlockSpec((GROUP, D), lambda i: (i, 0)),
        out_shape=jax.ShapeDtypeStruct(tokens.shape, jnp.bfloat16),
        compiler_params=pltpu.CompilerParams(vmem_limit_bytes=56 * 1024 * 1024),
        cost_estimate=pl.CostEstimate(
            flops=tokens.shape[0] * D * (3 * ff + 2 * GROUP),
            bytes_accessed=4 * tokens.size + 6 * D * ff,
            transcendentals=tokens.shape[0] * ff // 2,
        ),
    )(gates, slots, tokens, weights, down)


def scatter_sum_kernel(term_ref, out_ref, held, own, first, second, from_z, load_sem, core_send,
                       core_recv, first_send, first_recv, second_send, second_recv, z_send, z_recv):
    ctx, exp = lax.axis_index("ctx"), lax.axis_index("exp")
    z, core = ctx // 2, ctx % 2
    y, x = exp // 2, exp % 2
    beside_x, beside_y = y * 2 + (1 - x), (1 - y) * 2 + x
    owners = (exp, beside_x, beside_y, (1 - y) * 2 + (1 - x))
    sibling = (z * 2 + (1 - core), exp)
    plane_peer = ((ctx, beside_x), (ctx, beside_y))
    z_of = [(z + 1 + k) % 4 for k in range(4)]
    z_peer = [(z_of[k] * 2 + core, exp) for k in range(3)]
    rows, width = out_ref.shape
    half = width // 2
    columns = (pl.ds(0, half), pl.ds(half, half))
    piece = min(rows, 32)

    def remote(source, target, send, recv, device):
        return pltpu.make_async_remote_copy(
            src_ref=source, dst_ref=target, send_sem=send, recv_sem=recv,
            device_id=device, device_id_type=pl.DeviceIdType.MESH,
        )

    def add_rows(target, one, other):
        def some(i, carry):
            part = pl.ds(pl.multiple_of(i * piece, piece), piece)
            target[part, :] = one[part, :] + other[part, :]
            return carry

        lax.fori_loop(0, rows // piece, some, 0)

    barrier = pltpu.get_barrier_semaphore()
    partners = (sibling,) + plane_peer + tuple(z_peer)
    for device in partners:
        pl.semaphore_signal(barrier, inc=1, device_id=device, device_id_type=pl.DeviceIdType.MESH)
    pl.semaphore_wait(barrier, len(partners))

    loads, core_copies, first_copies, second_copies, z_copies = {}, {}, {}, {}, {}
    for k in range(4):
        for r in (3, 1, 2, 0):
            slot = k * 4 + r
            block = (z_of[k] * 2) * 4 + owners[r]
            core_copies[slot] = remote(
                term_ref.at[block + (1 - core) * 4], held.at[slot],
                core_send.at[slot], core_recv.at[slot], sibling,
            )
            core_copies[slot].start()
            loads[slot] = pltpu.make_async_copy(
                term_ref.at[block + core * 4], own.at[slot], load_sem.at[slot]
            )
            loads[slot].start()

    def send_first(k, h, j, r):
        index = k * 4 + h * 2 + j
        first_copies[index] = remote(
            held.at[k * 4 + r, :, columns[h]], first.at[index],
            first_send.at[index], first_recv.at[index], plane_peer[h],
        )
        first_copies[index].start()

    def over_core(k):
        for r in (3, 1, 2, 0):
            slot = k * 4 + r
            core_copies[slot].wait_recv()
            loads[slot].wait()
            add_rows(held.at[slot], held.at[slot], own.at[slot])
            if r == 3:
                send_first(k, 0, 1, 3)
                send_first(k, 1, 1, 3)
            elif r == 1:
                send_first(k, 0, 0, 1)
            elif r == 2:
                send_first(k, 1, 0, 2)

    def over_first(k):
        for h in range(2):
            index = k * 4 + h * 2 + 1
            first_copies[index].wait_recv()
            mine = held.at[k * 4 + 2 - h, :, columns[h]]
            add_rows(first.at[index], first.at[index], mine)
            place = k * 2 + h
            second_copies[place] = remote(
                first.at[index], second.at[place],
                second_send.at[place], second_recv.at[place], plane_peer[1 - h],
            )
            second_copies[place].start()
        for h in range(2):
            index = k * 4 + h * 2
            first_copies[index].wait_recv()
            add_rows(first.at[index], first.at[index], held.at[k * 4, :, columns[h]])

    def over_second(k):
        for h in range(2):
            second_copies[k * 2 + h].wait_recv()
            total = own.at[k * 4, :, columns[h]]
            add_rows(total, first.at[k * 4 + h * 2], second.at[k * 2 + h])
        if k < 3:
            z_copies[k] = remote(
                own.at[k * 4], from_z.at[k], z_send.at[k], z_recv.at[k], z_peer[k]
            )
            z_copies[k].start()

    for step in range(6):
        if step < 4:
            over_core(step)
        if 1 <= step < 5:
            over_first(step - 1)
        if step >= 2:
            over_second(step - 2)

    for k in range(3):
        z_copies[k].wait_recv()

    def finish(i, carry):
        part = pl.ds(pl.multiple_of(i * piece, piece), piece)
        total = own[12, part, :].astype(jnp.float32)
        for k in range(3):
            total += from_z[k, part, :].astype(jnp.float32)
        out_ref[part, :] = total.astype(jnp.bfloat16)
        return carry

    lax.fori_loop(0, rows // piece, finish, 0)
    for copies in (core_copies, first_copies, second_copies, z_copies):
        for copy in copies.values():
            copy.wait_send()


def scatter_sum(terms):
    rows, width = terms.shape[1:]
    return pl.pallas_call(
        scatter_sum_kernel,
        out_shape=jax.ShapeDtypeStruct((rows, width), jnp.bfloat16),
        in_specs=[pl.BlockSpec(memory_space=pl.ANY)],
        out_specs=pl.BlockSpec(memory_space=pltpu.VMEM),
        scratch_shapes=[
            pltpu.VMEM((16, rows, width), jnp.bfloat16),
            pltpu.VMEM((16, rows, width), jnp.bfloat16),
            pltpu.VMEM((16, rows, width // 2), jnp.bfloat16),
            pltpu.VMEM((8, rows, width // 2), jnp.bfloat16),
            pltpu.VMEM((3, rows, width), jnp.bfloat16),
        ]
        + [pltpu.SemaphoreType.DMA((n,)) for n in (16, 16, 16, 16, 16, 8, 8, 3, 3)],
        compiler_params=pltpu.CompilerParams(
            collective_id=0, has_side_effects=True, vmem_limit_bytes=58 * 1024 * 1024
        ),
        cost_estimate=pl.CostEstimate(
            flops=2 * terms.size, bytes_accessed=2 * terms.size, transcendentals=0
        ),
    )(terms)


def gather_expert_kernel(tok_ref, gate_ref, slot_ref, weight_ref, down_ref, term_ref,
                         held, upper, down, picked, out, own_sem, weight_sem, out_sem,
                         z_send, z_recv, side_send, side_recv, diag_send, diag_recv,
                         core_send, core_recv):
    ctx, exp = lax.axis_index("ctx"), lax.axis_index("exp")
    z, core = ctx // 2, ctx % 2
    y, x = exp // 2, exp % 2
    beside_x, beside_y = y * 2 + (1 - x), (1 - y) * 2 + x
    owners = (exp, beside_x, beside_y, (1 - y) * 2 + (1 - x))
    sibling = (z * 2 + (1 - core), exp)
    plane_peer = ((ctx, beside_x), (ctx, beside_y))
    z_peer = [(((z + k) % 4) * 2 + core, exp) for k in (1, 2, 3)]
    rows, width = tok_ref.shape
    chunk = min(width, 512)
    mine = pl.ds(pl.multiple_of(core * rows, rows), rows)
    theirs = pl.ds(pl.multiple_of((1 - core) * rows, rows), rows)

    def remote(source, target, send, recv, device):
        return pltpu.make_async_remote_copy(
            src_ref=source, dst_ref=target, send_sem=send, recv_sem=recv,
            device_id=device, device_id_type=pl.DeviceIdType.MESH,
        )

    def z_copy(k):
        return remote(tok_ref, held.at[k * 4, mine], z_send.at[k - 1], z_recv.at[k - 1],
                      z_peer[k - 1])

    def z_arrival(k):
        return remote(tok_ref, held.at[k * 4, mine], z_send.at[k - 1], z_recv.at[k - 1],
                      z_peer[0])

    def side_copy(k, h):
        return remote(held.at[k * 4, mine], held.at[k * 4 + 1 + h, mine],
                      side_send.at[k * 2 + h], side_recv.at[k * 2 + h], plane_peer[h])

    def diag_copy(k, h):
        half = pl.ds(pl.multiple_of(core * rows + h * (rows // 2), rows // 2), rows // 2)
        return remote(held.at[k * 4 + 2 - h, half], held.at[k * 4 + 3, half],
                      diag_send.at[k * 2 + h], diag_recv.at[k * 2 + h], plane_peer[h])

    def core_copy(k, r):
        slot = k * 4 + r
        return remote(held.at[slot, mine], held.at[slot, mine],
                      core_send.at[slot], core_recv.at[slot], sibling)

    def core_arrival(k, r):
        slot = k * 4 + r
        return remote(held.at[slot, theirs], held.at[slot, theirs],
                      core_send.at[slot], core_recv.at[slot], sibling)

    def out_copy(k, r, c):
        block = (((z - k + 4) % 4) * 2 + c) * 4 + owners[r]
        return pltpu.make_async_copy(
            out.at[r % 2, pl.ds(c * rows, rows)], term_ref.at[block], out_sem.at[r % 2, c]
        )

    upper_load = pltpu.make_async_copy(weight_ref.at[0, pl.ds(0, 2)], upper, weight_sem.at[0])
    down_load = pltpu.make_async_copy(down_ref, down, weight_sem.at[1])
    own_load = pltpu.make_async_copy(tok_ref, held.at[0, mine], own_sem)
    own_load.start()
    upper_load.start()
    down_load.start()

    barrier = pltpu.get_barrier_semaphore()
    partners = (sibling,) + plane_peer + tuple(z_peer)
    for device in partners:
        pl.semaphore_signal(barrier, inc=1, device_id=device, device_id_type=pl.DeviceIdType.MESH)
    pl.semaphore_wait(barrier, len(partners))

    def spread(k):
        side_copy(k, 0).start()
        side_copy(k, 1).start()
        core_copy(k, 0).start()

    own_load.wait()
    spread(0)
    for k in (1, 2, 3):
        z_copy(k).start()
    upper_load.wait()
    down_load.wait()

    def serve(k, r):
        slot = k * 4 + r
        core_arrival(k, r).wait_recv()
        if r >= 2:
            for c in range(2):
                out_copy(k, r - 2, c).wait()
        else:
            @pl.when(k > 0)
            def _():
                for c in range(2):
                    out_copy(k - 1, r + 2, c).wait()

        group = ((z - k + 4) % 4) * 4 + owners[r]
        chosen = slot_ref[group] == lax.broadcasted_iota(jnp.int32, (rows, 2 * rows), 0)
        row_gates = jnp.sum(jnp.where(chosen, gate_ref[group], 0.0), axis=1, keepdims=True)
        pick = chosen.astype(jnp.float32).astype(jnp.bfloat16)

        def take(i, carry):
            part = pl.ds(pl.multiple_of(i * chunk, chunk), chunk)
            picked[:, part] = jnp.dot(
                pick, held[slot, :, part], preferred_element_type=jnp.float32
            ).astype(jnp.bfloat16)
            return carry

        lax.fori_loop(0, width // chunk, take, 0)
        gate_part = jnp.dot(picked[...], upper[0], preferred_element_type=jnp.float32)
        upper_part = jnp.dot(picked[...], upper[1], preferred_element_type=jnp.float32)
        hidden = (gate_part / (1.0 + jnp.exp(-gate_part)) * upper_part).astype(jnp.bfloat16)

        def give(i, carry):
            part = pl.ds(pl.multiple_of(i * chunk, chunk), chunk)
            result = jnp.dot(hidden, down[:, part], preferred_element_type=jnp.float32)
            scaled = result.astype(jnp.bfloat16).astype(jnp.float32) * row_gates
            out[r % 2, :, part] = lax.dot_general(
                pick, scaled.astype(jnp.bfloat16), (((0,), (0,)), ((), ())),
                preferred_element_type=jnp.float32,
            ).astype(jnp.bfloat16)
            return carry

        lax.fori_loop(0, width // chunk, give, 0)
        for c in range(2):
            out_copy(k, r, c).start()

    def step(k, carry):
        serve(k, 0)
        side_copy(k, 0).wait_recv()
        diag_copy(k, 1).start()
        core_copy(k, 1).start()
        side_copy(k, 1).wait_recv()
        diag_copy(k, 0).start()
        core_copy(k, 2).start()

        @pl.when(k < 3)
        def _():
            z_arrival(k + 1).wait_recv()
            spread(k + 1)

        serve(k, 1)
        serve(k, 2)
        diag_copy(k, 0).wait_recv()
        diag_copy(k, 1).wait_recv()
        core_copy(k, 3).start()
        serve(k, 3)
        return carry

    lax.fori_loop(0, 4, step, 0)
    for r in (2, 3):
        for c in range(2):
            out_copy(3, r, c).wait()
    for k in (1, 2, 3):
        z_copy(k).wait_send()

    def drain(k, carry):
        for h in range(2):
            side_copy(k, h).wait_send()
            diag_copy(k, h).wait_send()
        for r in range(4):
            core_copy(k, r).wait_send()
        return carry

    lax.fori_loop(0, 4, drain, 0)


def gathered_terms(tokens, gates, slots, weights, down):
    rows, width = tokens.shape
    ff = weights.shape[-1]
    vmem = pl.BlockSpec(memory_space=pltpu.VMEM)
    hbm = pl.BlockSpec(memory_space=pl.ANY)
    return pl.pallas_call(
        gather_expert_kernel,
        out_shape=jax.ShapeDtypeStruct((32, rows, width), jnp.bfloat16),
        in_specs=[vmem, vmem, vmem, hbm, hbm],
        out_specs=hbm,
        scratch_shapes=[
            pltpu.VMEM((16, 2 * rows, width), jnp.bfloat16),
            pltpu.VMEM((2, width, ff), jnp.bfloat16),
            pltpu.VMEM((ff, width), jnp.bfloat16),
            pltpu.VMEM((rows, width), jnp.bfloat16),
            pltpu.VMEM((2, 2 * rows, width), jnp.bfloat16),
            pltpu.SemaphoreType.DMA,
            pltpu.SemaphoreType.DMA((2,)),
            pltpu.SemaphoreType.DMA((2, 2)),
        ]
        + [pltpu.SemaphoreType.DMA((n,)) for n in (3, 3, 8, 8, 8, 8, 16, 16)],
        compiler_params=pltpu.CompilerParams(
            collective_id=1, has_side_effects=True, vmem_limit_bytes=58 * 1024 * 1024
        ),
        cost_estimate=pl.CostEstimate(
            flops=32 * rows * width * (3 * ff + 4 * rows),
            bytes_accessed=64 * rows * width + 6 * width * ff,
            transcendentals=16 * rows * ff,
        ),
    )(tokens, gates, slots, weights, down)


def on_device(
    queries, keys, values, hidden_in, out_proj, norm_gain, route_ids, route_scores, expert_weights
):
    tok_rows = queries.shape[1]
    both = ("ctx", "exp")
    n_dev = lax.axis_size("ctx") * lax.axis_size("exp")
    gates = jax.nn.softmax(route_scores[0], -1)
    named = route_ids[0][None, :, :] == jnp.arange(n_dev, dtype=jnp.int32)[:, None, None]
    by_expert = jnp.sum(jnp.where(named, gates[None], 0.0), -1)
    by_expert = jnp.where(jnp.any(named, -1), by_expert, -1.0)
    my_gates = lax.all_to_all(by_expert, both, split_axis=0, concat_axis=0, tiled=True)
    down = expert_weights[0, 2].T

    kernel_mesh = (lax.axis_size("ctx"), lax.axis_size("exp")) == (8, 4)
    rounds = n_dev * tok_rows // ROUND_TOKENS
    part_rows = tok_rows // rounds
    groups = ROUND_TOKENS // GROUP
    if kernel_mesh:
        round_gates = my_gates.reshape(4, 2, 4, tok_rows).transpose(0, 2, 1, 3)
    else:
        round_gates = my_gates.reshape(n_dev, rounds, part_rows).transpose(1, 0, 2)
    round_gates = round_gates.reshape(rounds, groups, GROUP)
    mine = round_gates >= 0.0
    order = jnp.arange(GROUP)
    upto = (order[:, None] <= order[None, :]).astype(jnp.bfloat16)
    ranks = jnp.einsum(
        "rgt,tu->rgu", mine.astype(jnp.bfloat16), upto, preferred_element_type=jnp.float32
    )
    slots = jnp.where(mine, ranks.astype(jnp.int32) - 1, -1)[:, :, None, :]
    round_gates = round_gates[:, :, None, :]

    attended = attend(queries, keys, values)
    projected = jnp.dot(attended, out_proj, preferred_element_type=jnp.float32)
    residual = (hidden_in[0].astype(jnp.float32) + projected).astype(jnp.bfloat16)
    resid_f = residual.astype(jnp.float32)
    normed = (
        resid_f * lax.rsqrt(jnp.mean(resid_f * resid_f, -1, keepdims=True) + 1e-06) * norm_gain
    ).astype(jnp.bfloat16)

    def one_round(inputs):
        part, part_gates, part_slots = inputs
        tokens = lax.all_gather(part, both, axis=0, tiled=True)
        terms = expert_terms(tokens, part_gates, part_slots, expert_weights, down)
        return lax.psum_scatter(terms, both, scatter_dimension=0, tiled=True)

    parts = normed.reshape(rounds, part_rows, D)
    if kernel_mesh:
        terms = gathered_terms(normed, round_gates[0], slots[0], expert_weights, down)
        mixture = scatter_sum(terms)
    elif rounds == 1:
        mixture = one_round((parts[0], round_gates[0], slots[0]))
    else:
        mixture = lax.map(one_round, (parts, round_gates, slots)).reshape(tok_rows, D)
    layer_out = (resid_f + mixture.astype(jnp.float32)).astype(jnp.bfloat16)
    return (residual[None], layer_out[None])


def solution(mesh):
    return jax.shard_map(
        on_device,
        mesh=mesh,
        in_specs=(
            P("exp", "ctx", None),
            P("exp", "ctx", None),
            P("exp", "ctx", None),
            P("exp", "ctx", None),
            P(),
            P(),
            P("exp", "ctx", None),
            P("exp", "ctx", None),
            P(("ctx", "exp"), None, None, None),
        ),
        out_specs=(P("exp", "ctx", None), P("exp", "ctx", None)),
        check_vma=False,
    )
```
